1024 devices in a mesh: rep: 64 (over x, y, core), shard: 16 (over z).
Axes of the slice: x: 4, y: 8, z: 16, core: 2. Of those that a mesh axis runs over, the one named last changes fastest.
Arguments:
- tokens: bfloat16 [24576, 4096], P('rep'), may hold values from -70 to 70
- cotangent: bfloat16 [24576, 4096], P('rep', 'shard'), may hold values from -30 to 30
- moment_one: float32 [4096, 4096], P('rep', 'shard'), may hold values from -6 to 6
- moment_two: float32 [4096, 4096], P('rep', 'shard'), may hold values from 0.1 to 10
- master: float32 [4096, 4096], P('rep', 'shard'), may hold values from -0.09375 to 0.09375
Outputs:
- merged_grad: float32 [4096, 4096], P('rep', 'shard')
- new_moment_one: float32 [4096, 4096], P('rep', 'shard')
- new_moment_two: float32 [4096, 4096], P('rep', 'shard')
- new_master: float32 [4096, 4096], P('rep', 'shard')
- new_weights: bfloat16 [4096, 4096], P(None, 'shard')
The draws below stay inside these ranges and needn't reach their ends.
All inputs are finite; a program needn't handle non-finite values.
Results may differ from the reference program's by a relative error of at most 0.0004.
Values may be sent and summed in bfloat16 or wider, within the bound.
A program may use at most 64 MiB of HBM per device.

```python
import math
import jax
import jax.numpy as jnp

D = 4096
TOK_DEV = 384
STEP = 10
TOKENS = 24576
N_REP = 64


def draw_tokens(key, part):
    key = jax.random.fold_in(key, 11)
    keys = jax.random.split(key, 3)
    replicas = TOKENS // TOK_DEV
    shared = jnp.clip(jax.random.normal(keys[0], (TOK_DEV, D), jnp.float32), -4.0, 4.0)
    weight_shared = 0.6
    noise = jnp.clip(jax.random.normal(keys[1], (replicas, TOK_DEV, D), jnp.float32), -4.0, 4.0)
    feature = jnp.exp(jax.random.uniform(keys[2], (D,), jnp.float32, 0.0, math.log(10.0))) / 3.0
    ramp = 1.0 + 2.0 * jnp.arange(replicas, dtype=jnp.float32) / max(replicas - 1, 1)
    values = (weight_shared * shared[None] + noise) * feature * ramp[:, None, None]
    return values.reshape(TOKENS, D).astype(jnp.bfloat16)


def draw_cotangent(key, part):
    key = jax.random.fold_in(key, 23)
    keys = jax.random.split(key, 3)
    replicas = TOKENS // TOK_DEV
    shared = jnp.clip(jax.random.normal(keys[0], (TOK_DEV, D), jnp.float32), -4.0, 4.0)
    weight_shared = 0.6
    noise = jnp.clip(jax.random.normal(keys[1], (replicas, TOK_DEV, D), jnp.float32), -4.0, 4.0)
    rough = jnp.exp(jax.random.uniform(keys[2], (D,), jnp.float32, 0.0, math.log(10.0))) / 3.0
    column = rough * jnp.exp(math.log(3.0) * jnp.arange(D, dtype=jnp.float32) / D)
    values = (weight_shared * shared[None] + noise) * column / math.sqrt(TOK_DEV)
    return values.reshape(TOKENS, D).astype(jnp.bfloat16)


def steps_of(rng, extent, cuts, smallest, high):
    loudness = 1.0
    for position, parts in cuts:
        draws = jax.random.uniform(jax.random.fold_in(jax.random.fold_in(rng, 6), position), (parts,), jnp.float32, smallest / len(cuts), high / len(cuts))
        loudness = loudness * jnp.repeat(jnp.exp(draws), extent[position] // parts).reshape((-1,) + (1,) * (len(extent) - 1 - position))
    return loudness


def bell_draw(rng, shape, deviation, bound, cuts=(), kind=jnp.bfloat16):
    loudness = steps_of(rng, shape, cuts, -0.22, 0.18) if cuts else 1.0
    result = jax.random.normal(rng, shape, jnp.float32) * deviation * loudness
    return jnp.minimum(jnp.maximum(result, -bound), bound).astype(kind)


def setup_inputs(seed: int = 0) -> dict:
    key_of = jax.random.split(jax.random.key(seed), 6)
    return {
        "tokens": draw_tokens(jax.random.fold_in(key_of[5], 71), 0),
        "cotangent": draw_cotangent(jax.random.fold_in(key_of[5], 71), 0),
        "moment_one": bell_draw(key_of[2], (D, D), 1.0, 6.0, ((0, 64), (1, 16)), jnp.float32),
        "moment_two": jnp.clip(jnp.exp(math.log(10.0) - 4.6051702 * jax.random.uniform(key_of[3], (D, D), jnp.float32) ** steps_of(key_of[3], (D, D), ((0, 64), (1, 16)), -0.2, 0.2)), 0.1, 10.0),
        "master": bell_draw(key_of[4], (D, D), D ** -0.5, 0.09375, ((0, 64), (1, 16)), jnp.float32),
    }


def adasum_pair(first, second):
    aa = jnp.sum(first * first)
    bb = jnp.sum(second * second)
    ab = jnp.sum(first * second)
    return (1.0 - ab / (2.0 * (aa + 1e-06))) * first + (1.0 - ab / (2.0 * (bb + 1e-06))) * second

def reference(tokens, cotangent, moment_one, moment_two, master):

    def replica_grad(index):
        rows = tokens[index * TOK_DEV:(index + 1) * TOK_DEV]
        cot_rows = cotangent[index * TOK_DEV:(index + 1) * TOK_DEV]
        return jnp.dot(rows.T, cot_rows, preferred_element_type=jnp.float32)

    def subtree(offset, stride):
        if stride >= N_REP:
            return replica_grad(offset)
        left = subtree(offset, 2 * stride)
        right = subtree(offset + stride, 2 * stride)
        return adasum_pair(left, right)
    merged_grad = subtree(0, 1)
    new_one = 0.9 * moment_one + 0.1 * merged_grad
    new_two = 0.999 * moment_two + 0.001 * merged_grad * merged_grad
    first_fix = 1.0 - 0.9 ** STEP
    second_fix = 1.0 - 0.999 ** STEP
    update = new_one / first_fix / (jnp.sqrt(new_two / second_fix) + 1e-08) + 0.1 * master
    new_master = master - 0.001 * update
    return (merged_grad, new_one, new_two, new_master, new_master.astype(jnp.bfloat16))
```

```python
import functools

import jax
import jax.numpy as jnp
from jax import lax
from jax.experimental import pallas as pl
from jax.experimental.pallas import tpu as pltpu
from jax.sharding import PartitionSpec as P

STEP = 10
CORES = 2
CHIPS_Y = 8
TILES = 4
HEAD = 16
TOP = 2.0**15.75
TINY = 2.0**-126
MESH = pl.DeviceIdType.MESH


def encode(block, ref):
    rows = block.shape[0]
    for half in range(2):
        part = block[:, half * 128 : half * 128 + 128]
        peak = jnp.max(jnp.abs(part), axis=0, keepdims=True)
        scale = (peak * 1.01 + 1e-30).astype(jnp.bfloat16)
        unit = part * (TOP / scale.astype(jnp.float32))
        power = unit * unit
        power = power * power
        power = power * power
        power = jnp.where(part < 0.0, -power, power)
        ref[half * rows : half * rows + rows, :] = power.astype(jnp.bfloat16)
        ref[2 * rows + half * 8 : 2 * rows + half * 8 + 8, :] = jnp.broadcast_to(
            scale.astype(jnp.float32), (8, 128)
        ).astype(jnp.bfloat16)


def decode(ref, rows, half):
    scale = ref[2 * rows : 2 * rows + HEAD, :].astype(jnp.float32)
    scale = scale[half * 8 : half * 8 + 1, :] * (1.0 / TOP)
    coded = ref[half * rows : half * rows + rows, :].astype(jnp.float32)
    size = lax.rsqrt(lax.rsqrt(jnp.maximum(jnp.abs(coded), TINY)))
    value = size * lax.rsqrt(size) * scale
    return jnp.where(coded < 0.0, -value, value)


def pair_sums(data, sums, n, rows, first):
    width = max(n, 8)
    block = min(n, 4)
    for qb in range(0, n, block):
        for sb in range(qb, n, block):
            pairs = [
                (q, s)
                for q in range(qb, qb + block)
                for s in range(sb, sb + block)
                if q <= s
            ]

            def step(i, totals):
                at = pl.ds(pl.multiple_of(i * 8, 8), 8)
                out = list(totals)
                for half in range(2):
                    lanes = pl.ds(half * 128, 128)
                    item = {k: data[k, at, lanes] for k in {k for p in pairs for k in p}}
                    out = [o + item[q] * item[s] for o, (q, s) in zip(out, pairs)]
                return tuple(out)

            zero = jnp.zeros((8, 128), jnp.float32)
            totals = lax.fori_loop(0, rows // 8, step, (zero,) * len(pairs), unroll=2)
            for total, (q, s) in zip(totals, pairs):
                for a, b in {(q, s), (s, q)}:
                    at = (b * width + a) * 8
                    if first:
                        sums[at : at + 8, :] = total
                    else:
                        sums[at : at + 8, :] += total


def packing(n):
    per_row = min(n, 128 // n)
    return per_row, n // per_row


def pack(sums, n):
    width = max(n, 8)
    per_row, count = packing(n)
    sub = lax.broadcasted_iota(jnp.int32, (width, 128), 0)
    lane = lax.broadcasted_iota(jnp.int32, (width, 128), 1)
    place = (sub % per_row) * n
    gram = jnp.zeros((width, 128), jnp.float32)
    for s in range(n):
        part = sums[pl.ds(s * width * 8, width, 8), :]
        for i in range(1, 8):
            part = part + sums[pl.ds(s * width * 8 + i, width, 8), :]
        total = jnp.sum(part, axis=1, keepdims=True)
        gram = gram + jnp.where((lane == place + s) & (sub < n), total, 0.0)
    if count == 1:
        return jnp.sum(gram, axis=0, keepdims=True)
    return jnp.concatenate(
        [
            jnp.sum(gram[k * per_row : (k + 1) * per_row, :], axis=0, keepdims=True)
            for k in range(count)
        ],
        axis=0,
    )


def unpack(packed, n):
    width = max(n, 8)
    per_row, count = packing(n)
    each = width // count
    pieces = []
    for k in range(count):
        row = jnp.broadcast_to(packed[k : k + 1, :], (each, 128))
        sub = lax.broadcasted_iota(jnp.int32, (each, 128), 0)
        piece = row
        for q in range(1, per_row):
            piece = jnp.where(sub == q, pltpu.roll(row, 128 - q * n, 1), piece)
        pieces.append(piece)
    gram = pieces[0] if count == 1 else jnp.concatenate(pieces, axis=0)
    sub = lax.broadcasted_iota(jnp.int32, (width, 128), 0)
    lane = lax.broadcasted_iota(jnp.int32, (width, 128), 1)
    return jnp.where((lane < n) & (sub < n), gram, 0.0)


def swap(value, bit, axis):
    index = lax.broadcasted_iota(jnp.int32, value.shape, axis)
    size = value.shape[axis]
    up = pltpu.roll(value, bit, axis)
    down = pltpu.roll(value, size - bit, axis)
    return jnp.where((index // bit) % 2 == 1, up, down)


def adasum_weights(gram, n):
    width = gram.shape[0]
    sub = lax.broadcasted_iota(jnp.int32, (width, 128), 0)
    lane = lax.broadcasted_iota(jnp.int32, (width, 128), 1)
    weight = jnp.ones((width, 128), jnp.float32)
    bit = n // 2
    while bit:
        own = jnp.where(lane == sub, gram, 0.0)
        other = jnp.where(lane == jnp.where((sub // bit) % 2 == 1, sub - bit, sub + bit), gram, 0.0)
        down = 1.0 - jnp.sum(other, axis=1, keepdims=True) / (
            2.0 * (jnp.sum(own, axis=1, keepdims=True) + 1e-06)
        )
        down = jnp.broadcast_to(down, (width, 128))
        weight = weight * down
        if bit > 1:
            across = 1.0 - jnp.sum(other, axis=0, keepdims=True) / (
                2.0 * (jnp.sum(own, axis=0, keepdims=True) + 1e-06)
            )
            across = jnp.broadcast_to(across, (width, 128))
            scaled = across * gram
            scaled = scaled + swap(scaled, bit, 1)
            scaled = down * scaled
            gram = scaled + swap(scaled, bit, 0)
        bit //= 2
    return weight


def kernel(
    chips_x, shards, tokens, cotangent, moment_one, moment_two, master,
    out_grad, out_one, out_two, out_master, out_weights,
    x_send, x_recv, terms, x_sums, y_send, y_recv, parts, y_sums,
    z_one, x_one, z_two, x_two, y_two,
    x_ssem, x_rsem, y_ssem, y_rsem,
    z1_ssem, z1_rsem, x1_ssem, x1_rsem, z2_ssem, z2_rsem, x2_ssem, x2_rsem, y2_ssem, y2_rsem,
    wy_ssem, wy_rsem, wx_ssem, wx_rsem, wc_ssem, wc_rsem,
):
    rank, z = lax.axis_index("rep"), lax.axis_index("shard")
    peers = out_weights.shape[1] * CORES
    chips_y = out_weights.shape[1]
    x, place = rank // peers, rank % peers
    y, core = place // CORES, place % CORES
    rows_x = terms.shape[1]
    rows = out_grad.shape[0]
    tile = rows_x // TILES

    def remote(src, dst, ssem, rsem, device):
        return pltpu.make_async_remote_copy(
            src_ref=src, dst_ref=dst, send_sem=ssem, recv_sem=rsem,
            device_id=device, device_id_type=MESH,
        )

    def at_x(i):
        return (i * peers + place, z)

    def at_place(i):
        return (x * peers + i, z)

    def at_z(i):
        return (rank, i)

    barrier = pltpu.get_barrier_semaphore()
    for me, count, device in ((x, chips_x, at_x), (place, peers, at_place), (z, shards, at_z)):

        def greet(d, _, me=me, count=count, device=device):
            pl.semaphore_signal(
                barrier, inc=1, device_id=device((me + d) % count), device_id_type=MESH
            )
            return 0

        lax.fori_loop(1, count, greet, 0)

    def gradient(owner, t):
        at = pl.multiple_of(owner * rows_x + t * tile, tile)
        return lax.dot_general(
            tokens[:, pl.ds(at, tile)], cotangent[...], (((0,), (0,)), ((), ())),
            preferred_element_type=jnp.float32,
        )

    def x_copy(d, t):
        to = (x + d) % chips_x
        return remote(
            x_send.at[d - 1, t], x_recv.at[x, t], x_ssem.at[d - 1, t], x_rsem.at[x, t], at_x(to)
        )

    for t in range(TILES):
        for d in range(1, chips_x):
            encode(gradient((x + d) % chips_x, t), x_send.at[d - 1, t])
            if t == 0 and d == 1:
                pl.semaphore_wait(barrier, chips_x + peers + shards - 3)
            x_copy(d, t).start()
    for t in range(TILES):
        terms[x, t * tile : t * tile + tile, :] = gradient(x, t)

    for t in range(TILES):
        for d in range(1, chips_x):
            source = (x + d) % chips_x
            remote(
                x_send.at[d - 1, t], x_recv.at[source, t],
                x_ssem.at[d - 1, t], x_rsem.at[source, t], at_x(source),
            ).wait_recv()
            for half in range(2):
                terms[source, t * tile : t * tile + tile, half * 128 : half * 128 + 128] = decode(
                    x_recv.at[source, t], tile, half
                )
        pair_sums(terms.at[:, pl.ds(t * tile, tile), :], x_sums, chips_x, tile, t == 0)

    def total(value, slots, ssem, rsem, me, count, device):
        slots[me] = value

        def copy(i, to):
            return remote(slots.at[i], slots.at[i], ssem.at[to], rsem.at[i], device(to))

        def send(d, _):
            copy(me, (me + d) % count).start()
            return 0

        def wait(d, _):
            other = (me + d) % count
            copy(other, other).wait_recv()
            return 0

        def done(d, _):
            copy(me, (me + d) % count).wait_send()
            return 0

        lax.fori_loop(1, count, send, 0)
        lax.fori_loop(1, count, wait, 0)
        result = slots[0]
        for i in range(1, count):
            result = result + slots[i]
        lax.fori_loop(1, count, done, 0)
        return result

    gram = pack(x_sums, chips_x)
    gram = total(gram, z_one, z1_ssem, z1_rsem, z, shards, at_z)
    gram = total(gram, x_one, x1_ssem, x1_rsem, x, chips_x, at_x)
    weight = adasum_weights(unpack(gram, chips_x), chips_x)

    def combine(ref, at, size, weight, n, half):
        lanes = pl.ds(half * 128, 128)
        value = weight[0:1, :] * ref[0, pl.ds(at, size), lanes]
        for k in range(1, n):
            value = value + weight[k : k + 1, :] * ref[k, pl.ds(at, size), lanes]
        return value

    def y_copy(to):
        return remote(
            y_send.at[to], y_recv.at[place], y_ssem.at[to], y_rsem.at[place], at_place(to)
        )

    def y_block(to):
        at = pl.multiple_of(to * rows, rows)
        return jnp.concatenate(
            [combine(terms, at, rows, weight, chips_x, half) for half in range(2)], axis=1
        )

    def y_start(d, _):
        to = (place + d) % peers
        encode(y_block(to), y_send.at[to])
        y_copy(to).start()
        return 0

    lax.fori_loop(1, peers, y_start, 0)
    parts[place] = y_block(place)

    def y_wait(d, _):
        source = (place + d) % peers
        remote(
            y_send.at[source], y_recv.at[source],
            y_ssem.at[source], y_rsem.at[source], at_place(source),
        ).wait_recv()
        for half in range(2):
            parts[source, :, pl.ds(half * 128, 128)] = decode(y_recv.at[source], rows, half)
        return 0

    lax.fori_loop(1, peers, y_wait, 0)
    pair_sums(parts, y_sums, peers, rows, True)
    gram = pack(y_sums, peers)
    gram = total(gram, z_two, z2_ssem, z2_rsem, z, shards, at_z)
    gram = total(gram, x_two, x2_ssem, x2_rsem, x, chips_x, at_x)
    gram = total(gram, y_two, y2_ssem, y2_rsem, place, peers, at_place)
    weight = adasum_weights(unpack(gram, peers), peers)

    for half in range(2):
        lanes = pl.ds(half * 128, 128)
        merged = combine(parts, 0, rows, weight, peers, half)
        new_one = 0.9 * moment_one[:, lanes] + 0.1 * merged
        new_two = 0.999 * moment_two[:, lanes] + 0.001 * merged * merged
        first_fix = 1.0 - 0.9**STEP
        second_fix = 1.0 - 0.999**STEP
        old = master[:, lanes]
        update = new_one / first_fix / (jnp.sqrt(new_two / second_fix) + 1e-08) + 0.1 * old
        new_master = old - 0.001 * update
        out_grad[:, lanes] = merged
        out_one[:, lanes] = new_one
        out_two[:, lanes] = new_two
        out_master[:, lanes] = new_master
        out_weights[x, y, core, :, lanes] = new_master.astype(jnp.bfloat16)

    def wy_copy(source, to):
        block = out_weights.at[x, source, core]
        return remote(
            block, block, wy_ssem.at[to], wy_rsem.at[source], (x * peers + to * CORES + core, z)
        )

    def wx_copy(source, to):
        block = out_weights.at[source, :, core]
        return remote(block, block, wx_ssem.at[to], wx_rsem.at[source], at_x(to))

    def wc_copy(source, which):
        block = out_weights.at[source, :, which]
        return remote(
            block, block, wc_ssem.at[source], wc_rsem.at[source], at_place(y * CORES + 1 - core)
        )

    for d in range(1, chips_y):
        wy_copy(y, (y + d) % chips_y).start()
    for d in range(1, chips_y):
        wy_copy((y + d) % chips_y, (y + d) % chips_y).wait_recv()
    for d in range(1, chips_x):
        wx_copy(x, (x + d) % chips_x).start()
    wc_copy(x, core).start()
    for d in range(1, chips_x):
        source = (x + d) % chips_x
        wx_copy(source, source).wait_recv()
        wc_copy(source, core).start()
    for i in range(chips_x):
        wc_copy(i, 1 - core).wait_recv()
    for i in range(chips_x):
        wc_copy(i, core).wait_send()
    for d in range(1, chips_x):
        wx_copy(x, (x + d) % chips_x).wait_send()
    for d in range(1, chips_y):
        wy_copy(y, (y + d) % chips_y).wait_send()
    for d in range(1, chips_x):
        for t in range(TILES):
            x_copy(d, t).wait_send()

    def y_done(d, _):
        y_copy((place + d) % peers).wait_send()
        return 0

    lax.fori_loop(1, peers, y_done, 0)


def body(chips_y, tokens, cotangent, moment_one, moment_two, master):
    shards = lax.axis_size("shard")
    ranks = lax.axis_size("rep")
    peers = chips_y * CORES
    chips_x = ranks // peers
    depth, wide = tokens.shape[1], cotangent.shape[1]
    rows_x, rows = depth // chips_x, depth // ranks
    tile = rows_x // TILES
    coded = jnp.bfloat16
    f32 = jnp.float32
    one = (packing(chips_x)[1], 128)
    two = (packing(peers)[1], 128)
    dma = pltpu.SemaphoreType.DMA
    block = jax.ShapeDtypeStruct((rows, wide), f32)
    vmem = pl.BlockSpec(memory_space=pltpu.VMEM)
    outs = pl.pallas_call(
        functools.partial(kernel, chips_x, shards),
        out_shape=(
            block, block, block, block,
            jax.ShapeDtypeStruct((chips_x, chips_y, CORES, rows, wide), jnp.bfloat16),
        ),
        in_specs=[vmem] * 5,
        out_specs=(vmem,) * 5,
        scratch_shapes=[
            pltpu.VMEM((chips_x - 1, TILES, 2 * tile + HEAD, 128), coded),
            pltpu.VMEM((chips_x, TILES, 2 * tile + HEAD, 128), coded),
            pltpu.VMEM((chips_x, rows_x, wide), f32),
            pltpu.VMEM((chips_x * max(chips_x, 8) * 8, 128), f32),
            pltpu.VMEM((peers, 2 * rows + HEAD, 128), coded),
            pltpu.VMEM((peers, 2 * rows + HEAD, 128), coded),
            pltpu.VMEM((peers, rows, wide), f32),
            pltpu.VMEM((peers * max(peers, 8) * 8, 128), f32),
            pltpu.VMEM((shards,) + one, f32),
            pltpu.VMEM((chips_x,) + one, f32),
            pltpu.VMEM((shards,) + two, f32),
            pltpu.VMEM((chips_x,) + two, f32),
            pltpu.VMEM((peers,) + two, f32),
            dma((chips_x - 1, TILES)), dma((chips_x, TILES)),
            dma((peers,)), dma((peers,)),
            dma((shards,)), dma((shards,)),
            dma((chips_x,)), dma((chips_x,)),
            dma((shards,)), dma((shards,)),
            dma((chips_x,)), dma((chips_x,)),
            dma((peers,)), dma((peers,)),
            dma((chips_y,)), dma((chips_y,)),
            dma((chips_x,)), dma((chips_x,)),
            dma((chips_x,)), dma((chips_x,)),
        ],
        compiler_params=pltpu.CompilerParams(
            collective_id=0, has_side_effects=True, vmem_limit_bytes=48 * 1024 * 1024
        ),
        cost_estimate=pl.CostEstimate(
            flops=2 * tokens.shape[0] * depth * wide,
            bytes_accessed=6 * 1024 * 1024,
            transcendentals=0,
        ),
    )(tokens, cotangent, moment_one, moment_two, master)
    return outs[:4] + (outs[4].reshape(depth, wide),)


def solution(mesh, chips_y=CHIPS_Y):
    return jax.shard_map(
        functools.partial(body, chips_y),
        mesh=mesh,
        in_specs=(
            P("rep", None),
            P("rep", "shard"),
            P("rep", "shard"),
            P("rep", "shard"),
            P("rep", "shard"),
        ),
        out_specs=(
            P("rep", "shard"),
            P("rep", "shard"),
            P("rep", "shard"),
            P("rep", "shard"),
            P(None, "shard"),
        ),
        check_vma=False,
    )
```

```python
import functools

import jax
import jax.numpy as jnp
from jax import lax
from jax.experimental import pallas as pl
from jax.experimental.pallas import tpu as pltpu
from jax.sharding import PartitionSpec as P

STEP = 10
CORES = 2
CHIPS_Y = 8
TILES = 4
HEAD = 16
TOP = 2.0**15.75
TINY = 2.0**-126
MESH = pl.DeviceIdType.MESH


def encode(block, ref):
    rows = block.shape[0]
    for half in range(2):
        part = block[:, half * 128 : half * 128 + 128]
        peak = jnp.max(jnp.abs(part), axis=0, keepdims=True)
        scale = (peak * 1.01 + 1e-30).astype(jnp.bfloat16)
        unit = part * (TOP / scale.astype(jnp.float32))
        power = unit * unit
        power = power * power
        power = power * power
        power = jnp.where(part < 0.0, -power, power)
        ref[half * rows : half * rows + rows, :] = power.astype(jnp.bfloat16)
        ref[2 * rows + half * 8 : 2 * rows + half * 8 + 8, :] = jnp.broadcast_to(
            scale.astype(jnp.float32), (8, 128)
        ).astype(jnp.bfloat16)


def decode(ref, rows, half):
    scale = ref[2 * rows : 2 * rows + HEAD, :].astype(jnp.float32)
    scale = scale[half * 8 : half * 8 + 1, :] * (1.0 / TOP)
    coded = ref[half * rows : half * rows + rows, :].astype(jnp.float32)
    size = lax.rsqrt(lax.rsqrt(jnp.maximum(jnp.abs(coded), TINY)))
    value = size * lax.rsqrt(size) * scale
    return jnp.where(coded < 0.0, -value, value)


def pair_sums(data, sums, n, rows, first):
    width = max(n, 8)
    block = min(n, 4)
    for qb in range(0, n, block):
        for sb in range(qb, n, block):
            pairs = [
                (q, s)
                for q in range(qb, qb + block)
                for s in range(sb, sb + block)
                if q <= s
            ]

            def step(i, totals):
                at = pl.ds(pl.multiple_of(i * 8, 8), 8)
                out = list(totals)
                for half in range(2):
                    lanes = pl.ds(half * 128, 128)
                    item = {k: data[k, at, lanes] for k in {k for p in pairs for k in p}}
                    out = [o + item[q] * item[s] for o, (q, s) in zip(out, pairs)]
                return tuple(out)

            zero = jnp.zeros((8, 128), jnp.float32)
            totals = lax.fori_loop(0, rows // 8, step, (zero,) * len(pairs), unroll=2)
            for total, (q, s) in zip(totals, pairs):
                for a, b in {(q, s), (s, q)}:
                    at = (b * width + a) * 8
                    if first:
                        sums[at : at + 8, :] = total
                    else:
                        sums[at : at + 8, :] += total


def packing(n):
    per_row = min(n, 128 // n)
    return per_row, n // per_row


def pack(sums, n):
    width = max(n, 8)
    per_row, count = packing(n)
    sub = lax.broadcasted_iota(jnp.int32, (width, 128), 0)
    lane = lax.broadcasted_iota(jnp.int32, (width, 128), 1)
    place = (sub % per_row) * n
    gram = jnp.zeros((width, 128), jnp.float32)
    for s in range(n):
        part = sums[pl.ds(s * width * 8, width, 8), :]
        for i in range(1, 8):
            part = part + sums[pl.ds(s * width * 8 + i, width, 8), :]
        total = jnp.sum(part, axis=1, keepdims=True)
        gram = gram + jnp.where((lane == place + s) & (sub < n), total, 0.0)
    if count == 1:
        return jnp.sum(gram, axis=0, keepdims=True)
    return jnp.concatenate(
        [
            jnp.sum(gram[k * per_row : (k + 1) * per_row, :], axis=0, keepdims=True)
            for k in range(count)
        ],
        axis=0,
    )


def unpack(packed, n):
    width = max(n, 8)
    per_row, count = packing(n)
    each = width // count
    pieces = []
    for k in range(count):
        row = jnp.broadcast_to(packed[k : k + 1, :], (each, 128))
        sub = lax.broadcasted_iota(jnp.int32, (each, 128), 0)
        piece = row
        for q in range(1, per_row):
            piece = jnp.where(sub == q, pltpu.roll(row, 128 - q * n, 1), piece)
        pieces.append(piece)
    gram = pieces[0] if count == 1 else jnp.concatenate(pieces, axis=0)
    sub = lax.broadcasted_iota(jnp.int32, (width, 128), 0)
    lane = lax.broadcasted_iota(jnp.int32, (width, 128), 1)
    return jnp.where((lane < n) & (sub < n), gram, 0.0)


def swap(value, bit, axis):
    index = lax.broadcasted_iota(jnp.int32, value.shape, axis)
    size = value.shape[axis]
    up = pltpu.roll(value, bit, axis)
    down = pltpu.roll(value, size - bit, axis)
    return jnp.where((index // bit) % 2 == 1, up, down)


def adasum_weights(gram, n):
    width = gram.shape[0]
    sub = lax.broadcasted_iota(jnp.int32, (width, 128), 0)
    lane = lax.broadcasted_iota(jnp.int32, (width, 128), 1)
    weight = jnp.ones((width, 128), jnp.float32)
    bit = n // 2
    while bit:
        own = jnp.where(lane == sub, gram, 0.0)
        other = jnp.where(lane == jnp.where((sub // bit) % 2 == 1, sub - bit, sub + bit), gram, 0.0)
        down = 1.0 - jnp.sum(other, axis=1, keepdims=True) / (
            2.0 * (jnp.sum(own, axis=1, keepdims=True) + 1e-06)
        )
        down = jnp.broadcast_to(down, (width, 128))
        weight = weight * down
        if bit > 1:
            across = 1.0 - jnp.sum(other, axis=0, keepdims=True) / (
                2.0 * (jnp.sum(own, axis=0, keepdims=True) + 1e-06)
            )
            across = jnp.broadcast_to(across, (width, 128))
            scaled = across * gram
            scaled = scaled + swap(scaled, bit, 1)
            scaled = down * scaled
            gram = scaled + swap(scaled, bit, 0)
        bit //= 2
    return weight


def kernel(
    chips_x, shards, tokens_in, cotangent_in, one_in, two_in, master_in,
    out_states, out_weights,
    tokens, cotangent, states, in_sem, side_sem,
    x_send, x_recv, terms, x_sums, y_send, y_recv, parts, y_sums,
    z_one, x_one, z_two, x_two, y_two,
    x_ssem, x_rsem, y_ssem, y_rsem,
    z1_ssem, z1_rsem, x1_ssem, x1_rsem, z2_ssem, z2_rsem, x2_ssem, x2_rsem, y2_ssem, y2_rsem,
    wa_ssem, wa_rsem, wb_ssem, wb_rsem, wc_ssem, wc_rsem,
):
    rank, z = lax.axis_index("rep"), lax.axis_index("shard")
    peers = out_weights.shape[1] * CORES
    chips_y = out_weights.shape[1]
    x, place = lax.div(rank, peers), lax.rem(rank, peers)
    y, core = lax.div(place, CORES), lax.rem(place, CORES)
    rows_x = terms.shape[1]
    rows = out_states.shape[1]
    tile = rows_x // TILES

    def remote(src, dst, ssem, rsem, device):
        return pltpu.make_async_remote_copy(
            src_ref=src, dst_ref=dst, send_sem=ssem, recv_sem=rsem,
            device_id=device, device_id_type=MESH,
        )

    def at_x(i):
        return (i * peers + place, z)

    def at_place(i):
        return (x * peers + i, z)

    def at_z(i):
        return (rank, i)

    order = [(d, t) for t in range(TILES) for d in range(1, chips_x)]
    order += [(0, t) for t in range(TILES)]

    def columns(d, t):
        return pl.ds(pl.multiple_of(lax.rem(x + d, chips_x) * rows_x + t * tile, tile), tile)

    def token_copy(d, t):
        part = columns(d, t)
        return pltpu.make_async_copy(tokens_in.at[:, part], tokens.at[:, part], in_sem.at[d, t])

    barrier = pltpu.get_barrier_semaphore()
    for me, count, device in ((z, shards, at_z), (x, chips_x, at_x), (place, peers, at_place)):

        def greet(d, _, me=me, count=count, device=device):
            pl.semaphore_signal(
                barrier, inc=1, device_id=device(lax.rem(me + d, count)), device_id_type=MESH
            )
            return 0

        lax.fori_loop(1, count, greet, 0)

    side = [pltpu.make_async_copy(cotangent_in, cotangent, side_sem.at[0])]
    for i, ref in enumerate((one_in, two_in, master_in)):
        side.append(pltpu.make_async_copy(ref, states.at[i], side_sem.at[i + 1]))
    side[0].start()
    for d, t in order:
        token_copy(d, t).start()
    for copy in side[1:]:
        copy.start()

    def gradient(d, t):
        token_copy(d, t).wait()
        return lax.dot_general(
            tokens[:, columns(d, t)], cotangent[...], (((0,), (0,)), ((), ())),
            preferred_element_type=jnp.float32,
        )

    def x_copy(d, t):
        to = lax.rem(x + d, chips_x)
        return remote(
            x_send.at[d - 1, t], x_recv.at[x, t], x_ssem.at[d - 1, t], x_rsem.at[x, t], at_x(to)
        )

    side[0].wait()
    for d, t in order:
        if d == 0:
            terms[x, t * tile : t * tile + tile, :] = gradient(d, t)
            continue
        encode(gradient(d, t), x_send.at[d - 1, t])
        if (d, t) == order[0]:
            pl.semaphore_wait(barrier, chips_x + peers + shards - 3)
        x_copy(d, t).start()

    for t in range(TILES):
        for d in range(1, chips_x):
            source = lax.rem(x + d, chips_x)
            remote(
                x_send.at[d - 1, t], x_recv.at[source, t],
                x_ssem.at[d - 1, t], x_rsem.at[source, t], at_x(source),
            ).wait_recv()
            for half in range(2):
                terms[source, t * tile : t * tile + tile, half * 128 : half * 128 + 128] = decode(
                    x_recv.at[source, t], tile, half
                )
        pair_sums(terms.at[:, pl.ds(t * tile, tile), :], x_sums, chips_x, tile, t == 0)

    def total(value, slots, ssem, rsem, me, count, device):
        slots[me] = value

        def copy(i, to):
            return remote(slots.at[i], slots.at[i], ssem.at[to], rsem.at[i], device(to))

        def send(d, _):
            copy(me, lax.rem(me + d, count)).start()
            return 0

        def wait(d, _):
            other = lax.rem(me + d, count)
            copy(other, other).wait_recv()
            return 0

        def done(d, _):
            copy(me, lax.rem(me + d, count)).wait_send()
            return 0

        lax.fori_loop(1, count, send, 0)
        lax.fori_loop(1, count, wait, 0)
        result = jnp.sum(slots[...], axis=0)
        lax.fori_loop(1, count, done, 0)
        return result

    gram = pack(x_sums, chips_x)
    gram = total(gram, z_one, z1_ssem, z1_rsem, z, shards, at_z)
    gram = total(gram, x_one, x1_ssem, x1_rsem, x, chips_x, at_x)
    weight = adasum_weights(unpack(gram, chips_x), chips_x)

    def combine(ref, at, size, weight, n, half):
        lanes = pl.ds(half * 128, 128)
        value = weight[0:1, :] * ref[0, pl.ds(at, size), lanes]
        for k in range(1, n):
            value = value + weight[k : k + 1, :] * ref[k, pl.ds(at, size), lanes]
        return value

    def y_copy(to):
        return remote(
            y_send.at[to], y_recv.at[place], y_ssem.at[to], y_rsem.at[place], at_place(to)
        )

    def y_block(to):
        at = pl.multiple_of(to * rows, rows)
        return jnp.concatenate(
            [combine(terms, at, rows, weight, chips_x, half) for half in range(2)], axis=1
        )

    def y_start(d, _):
        to = lax.rem(place + d, peers)
        encode(y_block(to), y_send.at[to])
        y_copy(to).start()
        return 0

    lax.fori_loop(1, peers, y_start, 0)
    parts[place] = y_block(place)

    def y_wait(d, _):
        source = lax.rem(place + d, peers)
        remote(
            y_send.at[source], y_recv.at[source],
            y_ssem.at[source], y_rsem.at[source], at_place(source),
        ).wait_recv()
        for half in range(2):
            parts[source, :, pl.ds(half * 128, 128)] = decode(y_recv.at[source], rows, half)
        return 0

    lax.fori_loop(1, peers, y_wait, 0)
    pair_sums(parts, y_sums, peers, rows, True)
    gram = pack(y_sums, peers)
    gram = total(gram, z_two, z2_ssem, z2_rsem, z, shards, at_z)
    gram = total(gram, x_two, x2_ssem, x2_rsem, x, chips_x, at_x)
    gram = total(gram, y_two, y2_ssem, y2_rsem, place, peers, at_place)
    weight = adasum_weights(unpack(gram, peers), peers)

    for copy in side[1:]:
        copy.wait()
    for half in range(2):
        lanes = pl.ds(half * 128, 128)
        merged = combine(parts, 0, rows, weight, peers, half)
        new_one = 0.9 * states[0, :, lanes] + 0.1 * merged
        new_two = 0.999 * states[1, :, lanes] + 0.001 * merged * merged
        first_fix = 1.0 - 0.9**STEP
        second_fix = 1.0 - 0.999**STEP
        old = states[2, :, lanes]
        update = new_one / first_fix / (jnp.sqrt(new_two / second_fix) + 1e-08) + 0.1 * old
        new_master = old - 0.001 * update
        out_states[0, :, lanes] = merged
        out_states[1, :, lanes] = new_one
        out_states[2, :, lanes] = new_two
        out_states[3, :, lanes] = new_master
        out_weights[x, y, core, :, lanes] = new_master.astype(jnp.bfloat16)

    class Stream:
        def __init__(self, index, start, size, swapped):
            self.index, self.part, self.swapped = index, pl.ds(start, size), swapped
            self.count = (chips_x, chips_y) if swapped else (chips_y, chips_x)
            self.me = (x, y) if swapped else (y, x)

        def block(self, i, j, which):
            i, j = (i, j) if self.swapped else (j, i)
            return out_weights.at[i, j, which, self.part]

        def device(self, i, j):
            i, j = (i, j) if self.swapped else (j, i)
            return (i * peers + j * CORES + core, z)

        def a(self, source, to):
            block = self.block(source, self.me[1], core)
            return remote(
                block, block, wa_ssem.at[self.index, to], wa_rsem.at[self.index, source],
                self.device(to, self.me[1]),
            )

        def b(self, first, second, to):
            block = self.block(first, second, core)
            return remote(
                block, block, wb_ssem.at[self.index, first, to],
                wb_rsem.at[self.index, first, second], self.device(self.me[0], to),
            )

        def c(self, first, second, which):
            block = self.block(first, second, which)
            return remote(
                block, block, wc_ssem.at[self.index, first, second],
                wc_rsem.at[self.index, first, second], at_place(y * CORES + 1 - core),
            )

        def others(self, axis):
            count = self.count[axis]
            near = sorted(range(1, count), key=lambda d: min(d, count - d))
            return [lax.rem(self.me[axis] + d, count) for d in near]

        def forward(self, first):
            for to in self.others(1):
                self.b(first, self.me[1], to).start()
            self.c(first, self.me[1], core).start()

        def start(self):
            for to in self.others(0):
                self.a(self.me[0], to).start()
            self.forward(self.me[0])

        def middle(self):
            for source in self.others(0):
                self.a(source, source).wait_recv()
                self.forward(source)

        def last(self):
            for second in self.others(1):
                for first in [self.me[0]] + self.others(0):
                    self.b(first, second, second).wait_recv()
                    self.c(first, second, core).start()

        def finish(self):
            for first in [self.me[0]] + self.others(0):
                for second in [self.me[1]] + self.others(1):
                    self.c(first, second, 1 - core).wait_recv()
                    self.c(first, second, core).wait_send()
                for to in self.others(1):
                    self.b(first, self.me[1], to).wait_send()
            for to in self.others(0):
                self.a(self.me[0], to).wait_send()

    first_rows = rows * 3 // 4 // 16 * 16
    streams = [Stream(0, 0, first_rows, False)]
    if rows > first_rows:
        streams.append(Stream(1, first_rows, rows - first_rows, True))
    for stage in ("start", "middle", "last", "finish"):
        for stream in streams[:: -1 if stage == "middle" else 1]:
            getattr(stream, stage)()

    for d in range(1, chips_x):
        for t in range(TILES):
            x_copy(d, t).wait_send()

    def y_done(d, _):
        y_copy(lax.rem(place + d, peers)).wait_send()
        return 0

    lax.fori_loop(1, peers, y_done, 0)


def body(chips_y, tokens, cotangent, moment_one, moment_two, master):
    shards = lax.axis_size("shard")
    ranks = lax.axis_size("rep")
    peers = chips_y * CORES
    chips_x = ranks // peers
    depth, wide = tokens.shape[1], cotangent.shape[1]
    rows_x, rows = depth // chips_x, depth // ranks
    tile = rows_x // TILES
    coded = jnp.bfloat16
    f32 = jnp.float32
    one = (packing(chips_x)[1], 128)
    two = (packing(peers)[1], 128)
    dma = pltpu.SemaphoreType.DMA
    most = max(chips_x, chips_y)
    anywhere = pl.BlockSpec(memory_space=pl.ANY)
    vmem = pl.BlockSpec(memory_space=pltpu.VMEM)
    states, weights = pl.pallas_call(
        functools.partial(kernel, chips_x, shards),
        out_shape=(
            jax.ShapeDtypeStruct((4, rows, wide), f32),
            jax.ShapeDtypeStruct((chips_x, chips_y, CORES, rows, wide), jnp.bfloat16),
        ),
        in_specs=[anywhere] * 5,
        out_specs=(vmem,) * 2,
        scratch_shapes=[
            pltpu.VMEM(tokens.shape, jnp.bfloat16),
            pltpu.VMEM(cotangent.shape, jnp.bfloat16),
            pltpu.VMEM((3, rows, wide), f32),
            dma((chips_x, TILES)), dma((4,)),
            pltpu.VMEM((chips_x - 1, TILES, 2 * tile + HEAD, 128), coded),
            pltpu.VMEM((chips_x, TILES, 2 * tile + HEAD, 128), coded),
            pltpu.VMEM((chips_x, rows_x, wide), f32),
            pltpu.VMEM((chips_x * max(chips_x, 8) * 8, 128), f32),
            pltpu.VMEM((peers, 2 * rows + HEAD, 128), coded),
            pltpu.VMEM((peers, 2 * rows + HEAD, 128), coded),
            pltpu.VMEM((peers, rows, wide), f32),
            pltpu.VMEM((peers * max(peers, 8) * 8, 128), f32),
            pltpu.VMEM((shards,) + one, f32),
            pltpu.VMEM((chips_x,) + one, f32),
            pltpu.VMEM((shards,) + two, f32),
            pltpu.VMEM((chips_x,) + two, f32),
            pltpu.VMEM((peers,) + two, f32),
            dma((chips_x - 1, TILES)), dma((chips_x, TILES)),
            dma((peers,)), dma((peers,)),
            dma((shards,)), dma((shards,)),
            dma((chips_x,)), dma((chips_x,)),
            dma((shards,)), dma((shards,)),
            dma((chips_x,)), dma((chips_x,)),
            dma((peers,)), dma((peers,)),
            dma((2, most)), dma((2, most)),
            dma((2, most, most)), dma((2, most, most)),
            dma((2, most, most)), dma((2, most, most)),
        ],
        compiler_params=pltpu.CompilerParams(
            collective_id=0, has_side_effects=True, vmem_limit_bytes=60 * 1024 * 1024
        ),
        cost_estimate=pl.CostEstimate(
            flops=2 * tokens.shape[0] * depth * wide,
            bytes_accessed=6 * 1024 * 1024,
            transcendentals=0,
        ),
    )(tokens, cotangent, moment_one, moment_two, master)
    block = jax.ShapeDtypeStruct((rows, wide), f32)
    return pl.pallas_call(
        hand_out,
        out_shape=(block,) * 4 + (jax.ShapeDtypeStruct((depth, wide), jnp.bfloat16),),
        in_specs=[vmem] * 2,
        out_specs=(anywhere,) * 5,
        scratch_shapes=[dma((5,))],
    )(states, weights.reshape(depth, wide))


def hand_out(states, weights, *refs):
    outs, sem = refs[:5], refs[5]
    copies = [pltpu.make_async_copy(states.at[i], outs[i], sem.at[i]) for i in range(4)]
    copies.insert(0, pltpu.make_async_copy(weights, outs[4], sem.at[4]))
    for copy in copies:
        copy.start()
    for copy in copies:
        copy.wait()


def solution(mesh, chips_y=CHIPS_Y):
    return jax.shard_map(
        functools.partial(body, chips_y),
        mesh=mesh,
        in_specs=(
            P("rep", None),
            P("rep", "shard"),
            P("rep", "shard"),
            P("rep", "shard"),
            P("rep", "shard"),
        ),
        out_specs=(
            P("rep", "shard"),
            P("rep", "shard"),
            P("rep", "shard"),
            P("rep", "shard"),
            P(None, "shard"),
        ),
        check_vma=False,
    )
```

```python
import functools

import jax
import jax.numpy as jnp
from jax import lax
from jax.experimental import pallas as pl
from jax.experimental.pallas import tpu as pltpu
from jax.sharding import PartitionSpec as P

STEP = 10
CORES = 2
CHIPS_Y = 8
TILES = 4
HEAD = 16
TOP = 2.0**15.75
TINY = 2.0**-126
MESH = pl.DeviceIdType.MESH


def encode(block, ref):
    rows = block.shape[0]
    for half in range(2):
        part = block[:, half * 128 : half * 128 + 128]
        peak = jnp.max(jnp.abs(part), axis=0, keepdims=True)
        scale = (peak * 1.01 + 1e-30).astype(jnp.bfloat16)
        unit = part * (TOP / scale.astype(jnp.float32))
        power = unit * unit
        power = power * power
        power = power * power
        power = jnp.where(part < 0.0, -power, power)
        ref[half * rows : half * rows + rows, :] = power.astype(jnp.bfloat16)
        ref[2 * rows + half * 8 : 2 * rows + half * 8 + 8, :] = jnp.broadcast_to(
            scale.astype(jnp.float32), (8, 128)
        ).astype(jnp.bfloat16)


def decode(ref, rows, half):
    scale = ref[2 * rows : 2 * rows + HEAD, :].astype(jnp.float32)
    scale = scale[half * 8 : half * 8 + 1, :] * (1.0 / TOP)
    coded = ref[half * rows : half * rows + rows, :].astype(jnp.float32)
    size = lax.rsqrt(lax.rsqrt(jnp.maximum(jnp.abs(coded), TINY)))
    value = size * lax.rsqrt(size) * scale
    return jnp.where(coded < 0.0, -value, value)


def pair_sums(data, sums, n, rows, first):
    width = max(n, 8)
    block = min(n, 4)
    for qb in range(0, n, block):
        for sb in range(qb, n, block):
            pairs = [
                (q, s)
                for q in range(qb, qb + block)
                for s in range(sb, sb + block)
                if q <= s
            ]

            def step(i, totals):
                at = pl.ds(pl.multiple_of(i * 8, 8), 8)
                out = list(totals)
                for half in range(2):
                    lanes = pl.ds(half * 128, 128)
                    item = {k: data[k, at, lanes] for k in {k for p in pairs for k in p}}
                    out = [o + item[q] * item[s] for o, (q, s) in zip(out, pairs)]
                return tuple(out)

            zero = jnp.zeros((8, 128), jnp.float32)
            totals = lax.fori_loop(0, rows // 8, step, (zero,) * len(pairs), unroll=2)
            for total, (q, s) in zip(totals, pairs):
                for a, b in {(q, s), (s, q)}:
                    at = (b * width + a) * 8
                    if first:
                        sums[at : at + 8, :] = total
                    else:
                        sums[at : at + 8, :] += total


def packing(n):
    per_row = min(n, 128 // n)
    return per_row, n // per_row


def pack(sums, n):
    width = max(n, 8)
    per_row, count = packing(n)
    sub = lax.broadcasted_iota(jnp.int32, (width, 128), 0)
    lane = lax.broadcasted_iota(jnp.int32, (width, 128), 1)
    place = (sub % per_row) * n
    gram = jnp.zeros((width, 128), jnp.float32)
    for s in range(n):
        part = sums[pl.ds(s * width * 8, width, 8), :]
        for i in range(1, 8):
            part = part + sums[pl.ds(s * width * 8 + i, width, 8), :]
        total = jnp.sum(part, axis=1, keepdims=True)
        gram = gram + jnp.where((lane == place + s) & (sub < n), total, 0.0)
    if count == 1:
        return jnp.sum(gram, axis=0, keepdims=True)
    return jnp.concatenate(
        [
            jnp.sum(gram[k * per_row : (k + 1) * per_row, :], axis=0, keepdims=True)
            for k in range(count)
        ],
        axis=0,
    )


def unpack(packed, n):
    width = max(n, 8)
    per_row, count = packing(n)
    each = width // count
    pieces = []
    for k in range(count):
        row = jnp.broadcast_to(packed[k : k + 1, :], (each, 128))
        sub = lax.broadcasted_iota(jnp.int32, (each, 128), 0)
        piece = row
        for q in range(1, per_row):
            piece = jnp.where(sub == q, pltpu.roll(row, 128 - q * n, 1), piece)
        pieces.append(piece)
    gram = pieces[0] if count == 1 else jnp.concatenate(pieces, axis=0)
    sub = lax.broadcasted_iota(jnp.int32, (width, 128), 0)
    lane = lax.broadcasted_iota(jnp.int32, (width, 128), 1)
    return jnp.where((lane < n) & (sub < n), gram, 0.0)


def swap(value, bit, axis):
    index = lax.broadcasted_iota(jnp.int32, value.shape, axis)
    size = value.shape[axis]
    up = pltpu.roll(value, bit, axis)
    down = pltpu.roll(value, size - bit, axis)
    return jnp.where((index // bit) % 2 == 1, up, down)


def adasum_weights(gram, n):
    width = gram.shape[0]
    sub = lax.broadcasted_iota(jnp.int32, (width, 128), 0)
    lane = lax.broadcasted_iota(jnp.int32, (width, 128), 1)
    weight = jnp.ones((width, 128), jnp.float32)
    bit = n // 2
    while bit:
        own = jnp.where(lane == sub, gram, 0.0)
        other = jnp.where(lane == jnp.where((sub // bit) % 2 == 1, sub - bit, sub + bit), gram, 0.0)
        down = 1.0 - jnp.sum(other, axis=1, keepdims=True) / (
            2.0 * (jnp.sum(own, axis=1, keepdims=True) + 1e-06)
        )
        down = jnp.broadcast_to(down, (width, 128))
        weight = weight * down
        if bit > 1:
            across = 1.0 - jnp.sum(other, axis=0, keepdims=True) / (
                2.0 * (jnp.sum(own, axis=0, keepdims=True) + 1e-06)
            )
            across = jnp.broadcast_to(across, (width, 128))
            scaled = across * gram
            scaled = scaled + swap(scaled, bit, 1)
            scaled = down * scaled
            gram = scaled + swap(scaled, bit, 0)
        bit //= 2
    return weight


def kernel(
    chips_x, shards, tokens_in, cotangent_in, one_in, two_in, master_in,
    out_states, out_weights,
    tokens, cotangent, states, in_sem, side_sem,
    x_send, x_recv, terms, x_sums, y_send, y_recv, parts, y_sums,
    z_one, x_one, z_two, x_two, y_two,
    raw_send, raw_recv, factors, raw_ssem, raw_rsem, f_ssem, f_rsem,
    x_ssem, x_rsem, y_ssem, y_rsem,
    z1_ssem, z1_rsem, x1_ssem, x1_rsem, z2_ssem, z2_rsem, x2_ssem, x2_rsem, y2_ssem, y2_rsem,
    wa_ssem, wa_rsem, wb_ssem, wb_rsem, wc_ssem, wc_rsem,
):
    rank, z = lax.axis_index("rep"), lax.axis_index("shard")
    peers = out_weights.shape[1] * CORES
    chips_y = out_weights.shape[1]
    x, place = lax.div(rank, peers), lax.rem(rank, peers)
    y, core = lax.div(place, CORES), lax.rem(place, CORES)
    rows_x = terms.shape[1]
    rows = out_states.shape[1]
    tile = rows_x // TILES
    per_tile = peers // TILES
    early = rows // 4
    late = rows - early

    def tile_of(t):
        return lax.rem(lax.div(place, per_tile) + t + core * (TILES - 2 * t), TILES)

    def remote(src, dst, ssem, rsem, device):
        return pltpu.make_async_remote_copy(
            src_ref=src, dst_ref=dst, send_sem=ssem, recv_sem=rsem,
            device_id=device, device_id_type=MESH,
        )

    def at_x(i):
        return (i * peers + place, z)

    def at_place(i):
        return (x * peers + i, z)

    def at_z(i):
        return (rank, i)

    order = [(d, t) for t in range(TILES) for d in range(1, chips_x)]
    order += [(0, t) for t in range(TILES)]

    def columns(d, t):
        return pl.ds(pl.multiple_of(lax.rem(x + d, chips_x) * rows_x + tile_of(t) * tile, tile), tile)

    def token_copy(d, t):
        part = columns(d, t)
        return pltpu.make_async_copy(tokens_in.at[:, part], tokens.at[:, part], in_sem.at[d, t])

    barrier = pltpu.get_barrier_semaphore()
    for me, count, device in ((z, shards, at_z), (x, chips_x, at_x), (place, peers, at_place)):

        def greet(d, _, me=me, count=count, device=device):
            pl.semaphore_signal(
                barrier, inc=1, device_id=device(lax.rem(me + d, count)), device_id_type=MESH
            )
            return 0

        lax.fori_loop(1, count, greet, 0)

    side = [pltpu.make_async_copy(cotangent_in, cotangent, side_sem.at[0])]
    for i, ref in enumerate((one_in, two_in, master_in)):
        side.append(pltpu.make_async_copy(ref, states.at[i], side_sem.at[i + 1]))
    side[0].start()
    for d, t in order:
        token_copy(d, t).start()
    for copy in side[1:]:
        copy.start()

    def gradient(d, t):
        token_copy(d, t).wait()
        return lax.dot_general(
            tokens[:, columns(d, t)], cotangent[...], (((0,), (0,)), ((), ())),
            preferred_element_type=jnp.float32,
        )

    def x_copy(d, t):
        to = lax.rem(x + d, chips_x)
        return remote(
            x_send.at[d - 1, t], x_recv.at[x, t], x_ssem.at[d - 1, t], x_rsem.at[x, t], at_x(to)
        )

    side[0].wait()
    for d, t in order:
        if d == 0:
            terms[x, pl.ds(pl.multiple_of(tile_of(t) * tile, tile), tile), :] = gradient(d, t)
            continue
        encode(gradient(d, t), x_send.at[d - 1, t])
        if (d, t) == order[0]:
            pl.semaphore_wait(barrier, chips_x + peers + shards - 3)
        x_copy(d, t).start()

    def raw_copy(to):
        return remote(
            raw_send.at[to], raw_recv.at[place], raw_ssem.at[to], raw_rsem.at[place], at_place(to)
        )

    def raw_start(to):
        at = pl.ds(pl.multiple_of(to * rows, rows), early)
        block = jnp.concatenate([terms[k, at, :] for k in range(chips_x)], axis=0)
        encode(block, raw_send.at[to])
        raw_copy(to).start()

    for t in range(TILES):
        part = pl.ds(pl.multiple_of(tile_of(t) * tile, tile), tile)
        for d in range(1, chips_x):
            source = lax.rem(x + d, chips_x)
            remote(
                x_send.at[d - 1, t], x_recv.at[source, t],
                x_ssem.at[d - 1, t], x_rsem.at[source, t], at_x(source),
            ).wait_recv()
            for half in range(2):
                terms[source, part, half * 128 : half * 128 + 128] = decode(
                    x_recv.at[source, t], tile, half
                )
        if t == TILES - 1:
            pair_sums(terms.at[:, part, :], x_sums, chips_x, tile, False)

        def raw_step(j, _, t=t):
            to = tile_of(t) * per_tile + j

            @pl.when(to != place)
            def _():
                raw_start(to)

            return 0

        lax.fori_loop(0, per_tile, raw_step, 0)
        if t < TILES - 1:
            pair_sums(terms.at[:, part, :], x_sums, chips_x, tile, t == 0)

    def total(value, slots, ssem, rsem, me, count, device):
        slots[me] = value

        def copy(i, to):
            return remote(slots.at[i], slots.at[i], ssem.at[to], rsem.at[i], device(to))

        def send(d, _):
            copy(me, lax.rem(me + d, count)).start()
            return 0

        def wait(d, _):
            other = lax.rem(me + d, count)
            copy(other, other).wait_recv()
            return 0

        def done(d, _):
            copy(me, lax.rem(me + d, count)).wait_send()
            return 0

        lax.fori_loop(1, count, send, 0)
        lax.fori_loop(1, count, wait, 0)
        result = jnp.sum(slots[...], axis=0)
        lax.fori_loop(1, count, done, 0)
        return result

    gram = pack(x_sums, chips_x)
    gram = total(gram, z_one, z1_ssem, z1_rsem, z, shards, at_z)
    gram = total(gram, x_one, x1_ssem, x1_rsem, x, chips_x, at_x)
    weight = adasum_weights(unpack(gram, chips_x), chips_x)

    def combine(ref, at, size, weight, n, half):
        lanes = pl.ds(half * 128, 128)
        value = weight[0:1, :] * ref[0, pl.ds(at, size), lanes]
        for k in range(1, n):
            value = value + weight[k : k + 1, :] * ref[k, pl.ds(at, size), lanes]
        return value

    def y_copy(to):
        return remote(
            y_send.at[to], y_recv.at[place], y_ssem.at[to], y_rsem.at[place], at_place(to)
        )

    def f_copy(to):
        return remote(
            factors.at[place], factors.at[place], f_ssem.at[to], f_rsem.at[place], at_place(to)
        )

    factors[place] = weight[:chips_x, :]

    def f_start(d, _):
        f_copy(lax.rem(place + d, peers)).start()
        return 0

    lax.fori_loop(1, peers, f_start, 0)

    def y_block(to, first, size):
        at = pl.multiple_of(to * rows + first, 16)
        return jnp.concatenate(
            [combine(terms, at, size, weight, chips_x, half) for half in range(2)], axis=1
        )

    def y_start(d, _):
        to = lax.rem(place + d, peers)
        encode(y_block(to, early, late), y_send.at[to])
        y_copy(to).start()
        return 0

    lax.fori_loop(1, peers, y_start, 0)
    parts[place] = y_block(place, 0, rows)

    def raw_wait(d, _):
        source = lax.rem(place + d, peers)
        remote(
            raw_send.at[source], raw_recv.at[source],
            raw_ssem.at[source], raw_rsem.at[source], at_place(source),
        ).wait_recv()
        remote(
            factors.at[source], factors.at[source],
            f_ssem.at[source], f_rsem.at[source], at_place(source),
        ).wait_recv()
        factor = factors[source]
        for half in range(2):
            value = decode(raw_recv.at[source], chips_x * early, half)
            mix = factor[0:1, :] * value[:early, :]
            for k in range(1, chips_x):
                mix = mix + factor[k : k + 1, :] * value[k * early : k * early + early, :]
            parts[source, :early, half * 128 : half * 128 + 128] = mix
        return 0

    lax.fori_loop(1, peers, raw_wait, 0)

    def y_wait(d, _):
        source = lax.rem(place + d, peers)
        remote(
            y_send.at[source], y_recv.at[source],
            y_ssem.at[source], y_rsem.at[source], at_place(source),
        ).wait_recv()
        for half in range(2):
            parts[source, early:, half * 128 : half * 128 + 128] = decode(
                y_recv.at[source], late, half
            )
        return 0

    lax.fori_loop(1, peers, y_wait, 0)
    pair_sums(parts, y_sums, peers, rows, True)
    gram = pack(y_sums, peers)
    gram = total(gram, z_two, z2_ssem, z2_rsem, z, shards, at_z)
    gram = total(gram, x_two, x2_ssem, x2_rsem, x, chips_x, at_x)
    gram = total(gram, y_two, y2_ssem, y2_rsem, place, peers, at_place)
    weight = adasum_weights(unpack(gram, peers), peers)

    for copy in side[1:]:
        copy.wait()
    for half in range(2):
        lanes = pl.ds(half * 128, 128)
        merged = combine(parts, 0, rows, weight, peers, half)
        new_one = 0.9 * states[0, :, lanes] + 0.1 * merged
        new_two = 0.999 * states[1, :, lanes] + 0.001 * merged * merged
        first_fix = 1.0 - 0.9**STEP
        second_fix = 1.0 - 0.999**STEP
        old = states[2, :, lanes]
        update = new_one / first_fix / (jnp.sqrt(new_two / second_fix) + 1e-08) + 0.1 * old
        new_master = old - 0.001 * update
        out_states[0, :, lanes] = merged
        out_states[1, :, lanes] = new_one
        out_states[2, :, lanes] = new_two
        out_states[3, :, lanes] = new_master
        out_weights[x, y, core, :, lanes] = new_master.astype(jnp.bfloat16)

    class Stream:
        def __init__(self, index, start, size, swapped):
            self.index, self.part, self.swapped = index, pl.ds(start, size), swapped
            self.count = (chips_x, chips_y) if swapped else (chips_y, chips_x)
            self.me = (x, y) if swapped else (y, x)

        def block(self, i, j, which):
            i, j = (i, j) if self.swapped else (j, i)
            return out_weights.at[i, j, which, self.part]

        def device(self, i, j):
            i, j = (i, j) if self.swapped else (j, i)
            return (i * peers + j * CORES + core, z)

        def a(self, source, to):
            block = self.block(source, self.me[1], core)
            return remote(
                block, block, wa_ssem.at[self.index, to], wa_rsem.at[self.index, source],
                self.device(to, self.me[1]),
            )

        def b(self, first, second, to):
            block = self.block(first, second, core)
            return remote(
                block, block, wb_ssem.at[self.index, first, to],
                wb_rsem.at[self.index, first, second], self.device(self.me[0], to),
            )

        def c(self, first, second, which):
            block = self.block(first, second, which)
            return remote(
                block, block, wc_ssem.at[self.index, first, second],
                wc_rsem.at[self.index, first, second], at_place(y * CORES + 1 - core),
            )

        def others(self, axis):
            count = self.count[axis]
            near = sorted(range(1, count), key=lambda d: min(d, count - d))
            return [lax.rem(self.me[axis] + d, count) for d in near]

        def forward(self, first):
            for to in self.others(1):
                self.b(first, self.me[1], to).start()
            self.c(first, self.me[1], core).start()

        def start(self):
            for to in self.others(0):
                self.a(self.me[0], to).start()
            self.forward(self.me[0])

        def middle(self):
            for source in self.others(0):
                self.a(source, source).wait_recv()
                self.forward(source)

        def last(self):
            for second in self.others(1):
                for first in [self.me[0]] + self.others(0):
                    self.b(first, second, second).wait_recv()
                    self.c(first, second, core).start()

        def finish(self):
            for first in [self.me[0]] + self.others(0):
                for second in [self.me[1]] + self.others(1):
                    self.c(first, second, 1 - core).wait_recv()
                    self.c(first, second, core).wait_send()
                for to in self.others(1):
                    self.b(first, self.me[1], to).wait_send()
            for to in self.others(0):
                self.a(self.me[0], to).wait_send()

    first_rows = rows * 3 // 4 // 16 * 16
    streams = [Stream(0, 0, first_rows, False)]
    if rows > first_rows:
        streams.append(Stream(1, first_rows, rows - first_rows, True))
    for stage in ("start", "middle", "last", "finish"):
        for stream in streams[:: -1 if stage == "middle" else 1]:
            getattr(stream, stage)()

    for d in range(1, chips_x):
        for t in range(TILES):
            x_copy(d, t).wait_send()

    def y_done(d, _):
        to = lax.rem(place + d, peers)
        y_copy(to).wait_send()
        raw_copy(to).wait_send()
        f_copy(to).wait_send()
        return 0

    lax.fori_loop(1, peers, y_done, 0)


def body(chips_y, tokens, cotangent, moment_one, moment_two, master):
    shards = lax.axis_size("shard")
    ranks = lax.axis_size("rep")
    peers = chips_y * CORES
    chips_x = ranks // peers
    depth, wide = tokens.shape[1], cotangent.shape[1]
    rows_x, rows = depth // chips_x, depth // ranks
    tile = rows_x // TILES
    early = rows // 4
    late = rows - early
    coded = jnp.bfloat16
    f32 = jnp.float32
    one = (packing(chips_x)[1], 128)
    two = (packing(peers)[1], 128)
    dma = pltpu.SemaphoreType.DMA
    most = max(chips_x, chips_y)
    anywhere = pl.BlockSpec(memory_space=pl.ANY)
    vmem = pl.BlockSpec(memory_space=pltpu.VMEM)
    states, weights = pl.pallas_call(
        functools.partial(kernel, chips_x, shards),
        out_shape=(
            jax.ShapeDtypeStruct((4, rows, wide), f32),
            jax.ShapeDtypeStruct((chips_x, chips_y, CORES, rows, wide), jnp.bfloat16),
        ),
        in_specs=[anywhere] * 5,
        out_specs=(vmem,) * 2,
        scratch_shapes=[
            pltpu.VMEM(tokens.shape, jnp.bfloat16),
            pltpu.VMEM(cotangent.shape, jnp.bfloat16),
            pltpu.VMEM((3, rows, wide), f32),
            dma((chips_x, TILES)), dma((4,)),
            pltpu.VMEM((chips_x - 1, TILES, 2 * tile + HEAD, 128), coded),
            pltpu.VMEM((chips_x, TILES, 2 * tile + HEAD, 128), coded),
            pltpu.VMEM((chips_x, rows_x, wide), f32),
            pltpu.VMEM((chips_x * max(chips_x, 8) * 8, 128), f32),
            pltpu.VMEM((peers, 2 * late + HEAD, 128), coded),
            pltpu.VMEM((peers, 2 * late + HEAD, 128), coded),
            pltpu.VMEM((peers, rows, wide), f32),
            pltpu.VMEM((peers * max(peers, 8) * 8, 128), f32),
            pltpu.VMEM((shards,) + one, f32),
            pltpu.VMEM((chips_x,) + one, f32),
            pltpu.VMEM((shards,) + two, f32),
            pltpu.VMEM((chips_x,) + two, f32),
            pltpu.VMEM((peers,) + two, f32),
            pltpu.VMEM((peers, 2 * chips_x * early + HEAD, 128), coded),
            pltpu.VMEM((peers, 2 * chips_x * early + HEAD, 128), coded),
            pltpu.VMEM((peers, chips_x, 128), f32),
            dma((peers,)), dma((peers,)), dma((peers,)), dma((peers,)),
            dma((chips_x - 1, TILES)), dma((chips_x, TILES)),
            dma((peers,)), dma((peers,)),
            dma((shards,)), dma((shards,)),
            dma((chips_x,)), dma((chips_x,)),
            dma((shards,)), dma((shards,)),
            dma((chips_x,)), dma((chips_x,)),
            dma((peers,)), dma((peers,)),
            dma((2, most)), dma((2, most)),
            dma((2, most, most)), dma((2, most, most)),
            dma((2, most, most)), dma((2, most, most)),
        ],
        compiler_params=pltpu.CompilerParams(
            collective_id=0, has_side_effects=True, vmem_limit_bytes=60 * 1024 * 1024
        ),
        cost_estimate=pl.CostEstimate(
            flops=2 * tokens.shape[0] * depth * wide,
            bytes_accessed=6 * 1024 * 1024,
            transcendentals=0,
        ),
    )(tokens, cotangent, moment_one, moment_two, master)
    block = jax.ShapeDtypeStruct((rows, wide), f32)
    return pl.pallas_call(
        hand_out,
        out_shape=(block,) * 4 + (jax.ShapeDtypeStruct((depth, wide), jnp.bfloat16),),
        in_specs=[vmem] * 2,
        out_specs=(anywhere,) * 5,
        scratch_shapes=[dma((5,))],
    )(states, weights.reshape(depth, wide))


def hand_out(states, weights, *refs):
    outs, sem = refs[:5], refs[5]
    copies = [pltpu.make_async_copy(states.at[i], outs[i], sem.at[i]) for i in range(4)]
    copies.insert(0, pltpu.make_async_copy(weights, outs[4], sem.at[4]))
    for copy in copies:
        copy.start()
    for copy in copies:
        copy.wait()


def solution(mesh, chips_y=CHIPS_Y):
    return jax.shard_map(
        functools.partial(body, chips_y),
        mesh=mesh,
        in_specs=(
            P("rep", None),
            P("rep", "shard"),
            P("rep", "shard"),
            P("rep", "shard"),
            P("rep", "shard"),
        ),
        out_specs=(
            P("rep", "shard"),
            P("rep", "shard"),
            P("rep", "shard"),
            P("rep", "shard"),
            P(None, "shard"),
        ),
        check_vma=False,
    )
```
